256 devices in a mesh: row: 16 (over x_lo, z), col: 16 (over y, x_hi, core).
Axes of the slice: x: 4 (x_hi: 2, x_lo: 2; x = x_hi * 2 + x_lo), y: 4, z: 8, core: 2. Of those that a mesh axis runs over, the one named last changes fastest.
Arguments:
- queries: bfloat16 [16384, 2048], P(('row', 'col')), may hold values from -5 to 5
- key_storage_rows: bfloat16 [16384, 512], P(('col', 'row')), may hold values from -5 to 5
- values: bfloat16 [16384, 512], P(('col', 'row')), may hold values from -6 to 6
- tile_mask: int32 [256, 256], replicated, may hold values from 0 to 1, as said below
- slot_order: int32 [256], replicated, may hold values from 0 to 255, each once
Outputs:
- attended: bfloat16 [16384, 2048], P(('row', 'col'))
- log_total: float32 [16, 16384], P(None, ('row', 'col'))
The draws below stay inside these ranges and needn't reach their ends.
Inputs may be any that keep to these rules, and one draw needn't show every extreme that they name: tile_mask is 1 on its diagonal, 0 above it, and 0 or 1 below it.
All inputs are finite; a program needn't handle non-finite values.
Results may differ from the reference program's by a relative error of at most 0.004.
Values may be sent and summed in bfloat16 or wider, within the bound.
No kernel may reach another device: no remote copies, remote signals or barrier semaphores. Data moves between devices by JAX's collectives and lax.ppermute only.
A program may use at most 128 MiB of HBM per device.

```python
import math
import jax
import jax.numpy as jnp
from jax import lax

QUERY_HEADS = 16
KEY_VALUE_HEADS = 4
HEAD_SIZE = 128
BLOCK_TOKENS = 64
NCH = 256
SEQUENCE_TOKENS = 16384
N_ROW = 16
N_COL = 16


def draw_key_storage_rows(key, part):
    key = jax.random.fold_in(key, 7)
    base_offset = jnp.clip(jax.random.normal(key, (SEQUENCE_TOKENS, KEY_VALUE_HEADS * HEAD_SIZE), jnp.float32), -5.0, 5.0)
    return base_offset.astype(jnp.bfloat16)


def draw_queries(key, part):
    key = jax.random.fold_in(key, 11)
    base_offset = jnp.clip(jax.random.normal(key, (SEQUENCE_TOKENS, QUERY_HEADS * HEAD_SIZE), jnp.float32), -5.0, 5.0)
    return base_offset.astype(jnp.bfloat16)


def draw_tile_mask(key, part):
    key = jax.random.fold_in(key, 3)
    coins = jax.random.randint(key, (NCH, NCH), 0, 2)
    first = jnp.arange(NCH)[:, None]
    second = jnp.arange(NCH)[None, :]
    return jnp.where(first == second, 1, jnp.where(second < first, coins, 0)).astype(jnp.int32)


def level_of(stream_key, extent, cuts, low, high):
    def one(axis_at, blocks):
        heights = jax.random.uniform(jax.random.fold_in(jax.random.fold_in(stream_key, 6), axis_at), (blocks,), jnp.float32, low / len(cuts), high / len(cuts))
        return jnp.repeat(jnp.exp(heights), extent[axis_at] // blocks).reshape((-1,) + (1,) * (len(extent) - axis_at - 1))

    loudness = one(*cuts[0])
    for cut in cuts[1:]:
        loudness = loudness * one(*cut)
    return loudness


def centred(own_key, extent, width, reach, shards=(), kind=jnp.bfloat16):
    result = width * jax.random.normal(own_key, extent, jnp.float32)
    if shards:
        result = result * level_of(own_key, extent, shards, -0.22, 0.18)
    return jnp.clip(result, -reach, reach).astype(kind)


def setup_inputs(seed: int = 0) -> dict:
    arg_keys = jax.random.split(jax.random.key(seed), 6)
    return {
        "queries": draw_queries(jax.random.fold_in(arg_keys[5], 71), 0),
        "key_storage_rows": draw_key_storage_rows(jax.random.fold_in(arg_keys[5], 71), 0),
        "values": centred(arg_keys[2], (SEQUENCE_TOKENS, KEY_VALUE_HEADS * HEAD_SIZE), 1.0, 6.0, ((0, 256),)),
        "tile_mask": draw_tile_mask(jax.random.fold_in(arg_keys[5], 71), 0),
        "slot_order": jax.random.permutation(arg_keys[4], NCH).astype(jnp.int32),
    }


def reference(queries, key_storage_rows, values, tile_mask, slot_order):
    group_width = QUERY_HEADS // KEY_VALUE_HEADS
    scale = 1.0 / math.sqrt(HEAD_SIZE)
    offsets = jnp.arange(BLOCK_TOKENS, dtype=jnp.int32)
    key_pos = (slot_order[:, None] * BLOCK_TOKENS + offsets[None, :]).reshape(SEQUENCE_TOKENS)
    key_head_rows = key_storage_rows.astype(jnp.float32).reshape(N_COL, N_ROW * BLOCK_TOKENS, KEY_VALUE_HEADS, HEAD_SIZE)
    value_head_rows = values.astype(jnp.float32).reshape(N_COL, N_ROW * BLOCK_TOKENS, KEY_VALUE_HEADS, HEAD_SIZE)

    def one_block(slot):
        start = (slot * BLOCK_TOKENS).astype(jnp.int32)
        query_vectors = lax.dynamic_slice_in_dim(queries, start, BLOCK_TOKENS, 0).astype(jnp.float32)
        query_vectors = query_vectors.reshape(BLOCK_TOKENS, KEY_VALUE_HEADS, group_width, HEAD_SIZE)
        own = slot_order[slot]
        q_pos = own * BLOCK_TOKENS + offsets
        tile_open = tile_mask[own][slot_order]
        allowed = (jnp.repeat(tile_open, BLOCK_TOKENS)[None, :] == 1) & (key_pos[None, :] <= q_pos[:, None])
        allowed = allowed.reshape(BLOCK_TOKENS, N_COL, N_ROW * BLOCK_TOKENS)
        scores = jnp.einsum('qhgd,ckhd->hgqck', query_vectors, key_head_rows) * scale
        scores = jnp.where(allowed[None, None], scores, jnp.float32(-1e+30))
        local_max = lax.optimization_barrier(jnp.max(scores, axis=-1))
        weights = jnp.where(allowed[None, None], jnp.exp(scores - local_max[..., None]), jnp.float32(0.0))
        denominator = lax.optimization_barrier(jnp.sum(weights, axis=-1))
        rounded = lax.optimization_barrier(weights.astype(jnp.bfloat16)).astype(jnp.float32)
        numerator = jnp.einsum('hgqck,ckhd->hgqcd', rounded, value_head_rows)
        global_max = lax.optimization_barrier(jnp.max(local_max, axis=-1))
        factor = jnp.exp(local_max - global_max[..., None])
        total_den = lax.optimization_barrier(jnp.sum(denominator * factor, axis=-1))
        total_num = lax.optimization_barrier(jnp.sum(numerator * factor[..., None], axis=3))
        output = (total_num / total_den[..., None]).transpose(2, 0, 1, 3).reshape(BLOCK_TOKENS, QUERY_HEADS * HEAD_SIZE)
        lse_rows = (global_max + jnp.log(total_den)).reshape(QUERY_HEADS, BLOCK_TOKENS)
        return (output.astype(jnp.bfloat16), lse_rows)
    attended, log_total = lax.map(one_block, jnp.arange(N_ROW * N_COL, dtype=jnp.int32))
    return (attended.reshape(SEQUENCE_TOKENS, QUERY_HEADS * HEAD_SIZE), log_total.transpose(1, 0, 2).reshape(QUERY_HEADS, SEQUENCE_TOKENS))
```

```python
import math

import jax
import jax.numpy as jnp
import numpy as np
from jax import lax
from jax.experimental import pallas as pl
from jax.experimental.pallas import tpu as pltpu
from jax.sharding import Mesh
from jax.sharding import PartitionSpec as P

AXES = ("xl", "z", "y", "xh", "core")
SIZES = (2, 8, 4, 2, 2)
HEAD = 128
BLOCK = 64
GROUP = 4
ROWS = GROUP * BLOCK
SCALE = 1.0 / math.sqrt(HEAD)
LOG2E_SCALE = math.log2(math.e) * SCALE
NEG = -1e30
LANES = 128
CNT, DIA, DST = 120, 121, 122
TAIL = 16
TILES = 8
UNROLL = 4
Z_ORDER = (0, 1, 7, 2, 6, 3, 5, 4)

VMEM = pl.BlockSpec(memory_space=pltpu.VMEM)
SMEM = pl.BlockSpec(memory_space=pltpu.SMEM)
ANY = pl.BlockSpec(memory_space=pl.ANY)
f32, bf16, i32 = jnp.float32, jnp.bfloat16, jnp.int32


def permute(array, move):
    pairs = []
    for i in range(256):
        xl, z, y, xh, c = (int(v) for v in np.unravel_index(i, SIZES))
        x, y, z, c = move(2 * xh + xl, y, z, c)
        pairs.append((i, int(np.ravel_multi_index((x % 2, z, y, x // 2, c), SIZES))))
    return lax.ppermute(array, AXES, pairs)


def shift_x(array, k):
    return permute(array, lambda x, y, z, c: ((x + k) % 4, y, z, c))


def shift_y(array, k):
    return permute(array, lambda x, y, z, c: (x, (y + k) % 4, z, c))


def shift_z(array, k):
    return permute(array, lambda x, y, z, c: (x, y, (z + k) % 8, c))


def swap_core(array):
    return permute(array, lambda x, y, z, c: (x, y, z, 1 - c))


def call(kernel, in_specs, out_shape, out_specs, scratch=(), flops=0, size=0):
    return pl.pallas_call(
        kernel,
        in_specs=in_specs,
        out_specs=out_specs,
        out_shape=out_shape,
        scratch_shapes=scratch,
        cost_estimate=pl.CostEstimate(flops=flops, bytes_accessed=size, transcendentals=0),
        compiler_params=pltpu.CompilerParams(vmem_limit_bytes=48 << 20),
    )


def prep_kernel(at, q_ref, k_ref, v_ref, *outs):
    for s in range(4):
        h = lax.rem(at[0] + s, 4)
        out = outs[s]
        for g in range(GROUP):
            start = pl.multiple_of(h * (GROUP * HEAD) + g * HEAD, HEAD)
            out[g * BLOCK : (g + 1) * BLOCK, :] = q_ref[:, pl.ds(start, HEAD)]
        start = pl.multiple_of(h * HEAD, HEAD)
        out[ROWS : ROWS + BLOCK, :] = k_ref[:, pl.ds(start, HEAD)]
        out[ROWS + BLOCK :, :] = v_ref[:, pl.ds(start, HEAD)]


def lists_kernel(at, mask_ref, order_ref, out_ref):
    x, y, z, c = at[0], at[1], at[2], at[3]
    slots = lax.broadcasted_iota(i32, (1, 256), 1)
    order = order_ref[...]

    def slot(x, y, z, c):
        return lax.rem(x, 2) * 128 + z * 16 + y * 4 + lax.div(x, 2) * 2 + c

    def kv_slot(x, y, z, c):
        return (y * 4 + lax.div(x, 2) * 2 + c) * 16 + lax.rem(x, 2) * 8 + z

    i = lax.broadcasted_iota(i32, (16, 1), 0)
    qx = lax.rem(x - lax.rem(i, 4) + 4, 4)
    qy = lax.rem(y - lax.div(i, 4) + 4, 4)
    q_slot = slot(qx, qy, z, c)
    j = lax.broadcasted_iota(i32, (64, 1), 0)
    piece = lax.div(j, 8)
    zs = jnp.zeros_like(piece)
    for n, k in enumerate(Z_ORDER):
        zs = jnp.where(piece == n, k, zs)
    kc = lax.rem(c + lax.rem(lax.div(j, 4), 2), 2)
    k_slot = kv_slot(lax.rem(x - lax.rem(j, 4) + 4, 4), y, lax.rem(z - zs + 8, 8), kc)

    def one_hot(slot_col):
        block = jnp.sum(jnp.where(slots == slot_col, order, 0), axis=1, keepdims=True)
        return jnp.where(slots == block, 1.0, 0.0).astype(bf16)

    q_hot, k_hot = one_hot(q_slot), one_hot(k_slot)
    rows = jnp.dot(q_hot, mask_ref[...].astype(f32).astype(bf16), preferred_element_type=f32)
    contract = (((1,), (1,)), ((), ()))
    opened = lax.dot_general(rows.astype(bf16), k_hot, contract, preferred_element_type=f32)
    same = lax.dot_general(q_hot, k_hot, contract, preferred_element_type=f32)
    off = opened * (1.0 - same)
    below = jnp.where(
        lax.broadcasted_iota(i32, (64, 64), 0) < lax.broadcasted_iota(i32, (64, 64), 1), 1.0, 0.0
    ).astype(bf16)
    rank = jnp.dot(off.astype(bf16), below, preferred_element_type=f32)
    n_off = jnp.sum(off, axis=1, keepdims=True)
    n_dia = jnp.sum(same, axis=1, keepdims=True)
    pos = jnp.where(same > 0.5, n_off, jnp.where(off > 0.5, rank, 999.0))
    lane = lax.broadcasted_iota(i32, (16, LANES), 1)
    lanes = lane.astype(f32)
    out = jnp.zeros((16, LANES), f32)
    for n in range(64):
        out = out + jnp.where(pos[:, n : n + 1] == lanes, float(n), 0.0)
    out = jnp.where(lane == CNT, n_off + n_dia, out)
    out = jnp.where(lane == DIA, n_dia, out)
    target = lax.rem(qx, 2) * 8 + qy * 2 + lax.div(qx, 2)
    out_ref[:16, :] = jnp.where(lane == DST, target, out.astype(i32))
    out_ref[16:, :] = jnp.zeros((8, LANES), i32)


def attend_kernel(info, *refs):
    q_in, kv_in = refs[:4], refs[4:20]
    o_ref = refs[20]
    q_s, kv_s, m_s, l_s, acc_s, work_q, work_g, sems = refs[21:]
    copies = []
    for t in range(4):
        copies.append((q_in[t], q_s.at[pl.ds(t * 4, 4)]))
    for n in range(16):
        copies.append((kv_in[n], kv_s.at[pl.ds(n * 4, 4)]))
    copies = [pltpu.make_async_copy(a, b, sems.at[n]) for n, (a, b) in enumerate(copies)]
    for copy in copies:
        copy.start()

    def fill(qb, t):
        def put(g, t):
            work_q[t] = qb
            work_g[t] = g * TILES
            return t + 1

        return lax.fori_loop(0, jnp.maximum(info[qb, CNT] - 1, 0) // TILES, put, t)

    items = lax.fori_loop(0, 16, fill, 0)
    for u in range(UNROLL - 1):
        work_q[items + u] = 16
        work_g[items + u] = 0
    for copy in copies:
        copy.wait()
    q_s[16] = q_s[0]

    row = lax.broadcasted_iota(i32, (BLOCK, ROWS), 0)
    ahead = row - lax.rem(lax.broadcasted_iota(i32, (BLOCK, ROWS), 1), BLOCK)

    def tiles(qb, base, part):
        rows = pl.ds(part * BLOCK, BLOCK)
        return jnp.concatenate([kv_s[info[qb, base + n], rows, :] for n in range(TILES)], axis=0)

    def scores(qb, base):
        return lax.dot_general(
            tiles(qb, base, 0), q_s[qb], (((1,), (1,)), ((), ())), preferred_element_type=f32
        )

    def weighted(qb, base, p):
        return lax.dot_general(
            tiles(qb, base, 1), p.astype(bf16), (((0,), (0,)), ((), ())), preferred_element_type=f32
        )

    def last(t, carry):
        for u in range(UNROLL):
            qb = t * UNROLL + u
            n, dia = info[qb, CNT], info[qb, DIA]
            base = jnp.maximum(n - 1, 0) // TILES * TILES
            s = scores(qb, base)
            parts = []
            for i in range(TILES):
                limit = jnp.where(base + i < n - dia, 1000, jnp.where(base + i < n, 0, -1000))
                parts.append(jnp.where(ahead <= limit, s[i * BLOCK : (i + 1) * BLOCK], NEG))
            s = jnp.concatenate(parts, axis=0)
            m = jnp.max(s, axis=0, keepdims=True) * LOG2E_SCALE
            p = jnp.exp2(s * LOG2E_SCALE - m)
            m_s[qb] = m
            l_s[qb] = jnp.where(n > 0, jnp.sum(p, axis=0, keepdims=True), 0.0)
            acc_s[qb] = weighted(qb, base, p)
        return carry

    lax.fori_loop(0, 16 // UNROLL, last, 0)

    def full(t, carry):
        for u in range(UNROLL):
            qb, base = work_q[t * UNROLL + u], work_g[t * UNROLL + u]
            p = jnp.exp2(scores(qb, base) * LOG2E_SCALE - m_s[qb])
            l_s[qb] += jnp.sum(p, axis=0, keepdims=True)
            acc_s[qb] += weighted(qb, base, p)
        return carry

    m_s[16] = jnp.zeros((1, ROWS), f32)
    lax.fori_loop(0, (items + UNROLL - 1) // UNROLL, full, 0)

    def safe(qb, carry):
        m0, l0, a0 = m_s[qb], l_s[qb], acc_s[qb]
        worst = jnp.max(l_s[qb])

        @pl.when(jnp.logical_not(worst < 1e30))
        def _():
            n, dia = info[qb, CNT], info[qb, DIA]

            def step(g, state):
                m, l, acc = state
                base = g * TILES
                s = scores(qb, base)
                parts = []
                for i in range(TILES):
                    limit = jnp.where(base + i < n - dia, 1000, jnp.where(base + i < n, 0, -1000))
                    parts.append(jnp.where(ahead <= limit, s[i * BLOCK : (i + 1) * BLOCK], NEG))
                s = jnp.concatenate(parts, axis=0)
                m_new = jnp.maximum(m, jnp.max(s, axis=0, keepdims=True) * LOG2E_SCALE)
                p = jnp.exp2(s * LOG2E_SCALE - m_new)
                fade = jnp.exp2(m - m_new)
                return (
                    m_new,
                    l * fade + jnp.sum(p, axis=0, keepdims=True),
                    acc * fade + weighted(qb, base, p),
                )

            start = (jnp.full_like(m0, NEG), jnp.zeros_like(l0), jnp.zeros_like(a0))
            m, l, acc = lax.fori_loop(0, (n + TILES - 1) // TILES, step, start)
            m_s[qb] = m
            l_s[qb] = l
            acc_s[qb] = acc

        return carry

    lax.fori_loop(0, 16, safe, 0)

    def finish(qb, carry):
        l = l_s[qb]
        some = l > 0
        target = info[qb, DST]
        o_ref[target, :HEAD, :] = (acc_s[qb] * jnp.where(some, 1.0 / l, 0.0)).astype(bf16)
        lse = jnp.where(some, m_s[qb] * math.log(2.0) + jnp.log(l), NEG)
        high = lse.astype(bf16).astype(f32)
        mid = (lse - high).astype(bf16).astype(f32)
        low = lse - high - mid
        at = lax.broadcasted_iota(i32, (TAIL, ROWS), 0)
        tail = jnp.where(at == 0, high, jnp.where(at == 1, mid, jnp.where(at == 2, low, 0.0)))
        o_ref[target, HEAD:, :] = tail.astype(bf16)
        return carry

    lax.fori_loop(0, 16, finish, 0)


def combine_kernel(in_ref, out_ref, lse_ref):
    for h in range(4):
        src = [(h % 2) * 8 + c * 2 + h // 2 for c in range(4)]
        lses = []
        for s in src:
            tail = in_ref[s, HEAD:, :].astype(f32)
            lses.append(tail[0:1] + tail[1:2] + tail[2:3])
        top = jnp.maximum(jnp.maximum(lses[0], lses[1]), jnp.maximum(lses[2], lses[3]))
        weights = [jnp.exp(lse - top) for lse in lses]
        total = weights[0] + weights[1] + weights[2] + weights[3]
        inverse = 1.0 / total
        o = sum(in_ref[s, :HEAD, :].astype(f32) * (w * inverse) for s, w in zip(src, weights))
        o = o.T.astype(bf16)
        lse = top + jnp.log(total)
        for g in range(GROUP):
            rows = slice(g * BLOCK, (g + 1) * BLOCK)
            head = h * GROUP + g
            out_ref[:, head * HEAD : (head + 1) * HEAD] = o[rows]
            lse_ref[head : head + 1, :] = lse[:, rows]


def body(queries, keys, values, tile_mask, slot_order):
    x = 2 * lax.axis_index("xh") + lax.axis_index("xl")
    at = jnp.stack([x, lax.axis_index("y"), lax.axis_index("z"), lax.axis_index("core")])
    at = at.astype(i32)

    with jax.named_scope("prep"):
        piece = jax.ShapeDtypeStruct((ROWS + 2 * BLOCK, HEAD), bf16)
        pieces = call(prep_kernel, [SMEM] + [VMEM] * 3, [piece] * 4, [VMEM] * 4)(
            at, queries, keys, values
        )
    with jax.named_scope("heads"):
        pieces = [pieces[0]] + [shift_x(pieces[s], s) for s in (1, 2, 3)]
        own_kv = jnp.stack([p[ROWS:] for p in pieces])
        own_q = jnp.stack([p[:ROWS] for p in pieces])
    with jax.named_scope("lists"):
        info = call(
            lists_kernel, [SMEM, VMEM, VMEM], jax.ShapeDtypeStruct((24, LANES), i32), VMEM
        )(at, tile_mask, slot_order.reshape(1, 256))
    with jax.named_scope("gather"):
        kv = {0: own_kv}
        for s in (1, 7, 2, 6):
            kv[s] = shift_z(own_kv, s)
        qs = [own_q] + [shift_y(own_q, t) for t in (1, 2, 3)]
        kv[3] = shift_z(kv[2], 1)
        kv[5] = shift_z(kv[6], 7)
        kv[4] = jnp.concatenate([shift_z(kv[2][:2], 2), shift_z(kv[6][2:], 6)])
        flat = []
        for s in Z_ORDER:
            flat += [kv[s], swap_core(kv[s])]
    with jax.named_scope("attend"):
        partial = call(
            attend_kernel,
            [SMEM] + [ANY] * 20,
            jax.ShapeDtypeStruct((16, HEAD + TAIL, ROWS), bf16),
            VMEM,
            [
                pltpu.VMEM((17, ROWS, HEAD), bf16),
                pltpu.VMEM((64, 2 * BLOCK, HEAD), bf16),
                pltpu.VMEM((17, 1, ROWS), f32),
                pltpu.VMEM((17, 1, ROWS), f32),
                pltpu.VMEM((17, HEAD, ROWS), f32),
                pltpu.SMEM((16 * 8 + UNROLL,), i32),
                pltpu.SMEM((16 * 8 + UNROLL,), i32),
                pltpu.SemaphoreType.DMA((20,)),
            ],
            flops=2_000_000_000,
            size=4_000_000,
        )(info, *qs, *flat)
    with jax.named_scope("exchange"):
        parts = lax.all_to_all(partial, ("xl", "y", "xh"), split_axis=0, concat_axis=0, tiled=True)
    with jax.named_scope("combine"):
        return call(
            combine_kernel,
            [VMEM],
            [jax.ShapeDtypeStruct((BLOCK, 16 * HEAD), bf16), jax.ShapeDtypeStruct((16, BLOCK), f32)],
            [VMEM, VMEM],
        )(parts)


def solution(mesh):
    fine = Mesh(mesh.devices.reshape(SIZES), AXES)
    by_query, by_key = AXES, ("y", "xh", "core", "xl", "z")
    return jax.shard_map(
        body,
        mesh=fine,
        in_specs=(P(by_query, None), P(by_key, None), P(by_key, None), P(), P()),
        out_specs=(P(by_query, None), P(None, by_query)),
        check_vma=False,
    )
```

```python
import functools
import math

import jax
import jax.numpy as jnp
import numpy as np
from jax import lax
from jax.experimental import pallas as pl
from jax.experimental.pallas import tpu as pltpu
from jax.sharding import Mesh
from jax.sharding import PartitionSpec as P

AXES = ("xl", "z", "y", "xh", "core")
SIZES = (2, 8, 4, 2, 2)
HEAD = 128
BLOCK = 64
GROUP = 4
ROWS = GROUP * BLOCK
SCALE = 1.0 / math.sqrt(HEAD)
LOG2E_SCALE = math.log2(math.e) * SCALE
NEG = -1e30
LANES = 128
CNT, DIA, DST = 120, 121, 122
TAIL = 16
TILES = 4
UNROLL = 8
NEAR = (0, 1, 7, 2, 6)
FAR = (3, 5, 4)
UNITS = [(k, c) for zs in (NEAR, FAR) for c in (0, 1) for k in zs]
SPLIT = 8 * len(NEAR)

VMEM = pl.BlockSpec(memory_space=pltpu.VMEM)
SMEM = pl.BlockSpec(memory_space=pltpu.SMEM)
ANY = pl.BlockSpec(memory_space=pl.ANY)
f32, bf16, i32 = jnp.float32, jnp.bfloat16, jnp.int32


def permute(array, move):
    pairs = []
    for i in range(256):
        xl, z, y, xh, c = (int(v) for v in np.unravel_index(i, SIZES))
        x, y, z, c = move(2 * xh + xl, y, z, c)
        pairs.append((i, int(np.ravel_multi_index((x % 2, z, y, x // 2, c), SIZES))))
    return lax.ppermute(array, AXES, pairs)


def shift_x(array, k):
    return permute(array, lambda x, y, z, c: ((x + k) % 4, y, z, c))


def shift_y(array, k):
    return permute(array, lambda x, y, z, c: (x, (y + k) % 4, z, c))


def shift_z(array, k):
    return permute(array, lambda x, y, z, c: (x, y, (z + k) % 8, c))


def swap_core(array):
    return permute(array, lambda x, y, z, c: (x, y, z, 1 - c))


def call(kernel, in_specs, out_shape, out_specs, scratch=(), flops=0, size=0, limit=48):
    return pl.pallas_call(
        kernel,
        in_specs=in_specs,
        out_specs=out_specs,
        out_shape=out_shape,
        scratch_shapes=scratch,
        cost_estimate=pl.CostEstimate(flops=flops, bytes_accessed=size, transcendentals=0),
        compiler_params=pltpu.CompilerParams(vmem_limit_bytes=limit << 20),
    )


def place():
    x = 2 * lax.axis_index("xh") + lax.axis_index("xl")
    return x, lax.axis_index("y"), lax.axis_index("z"), lax.axis_index("core")


def prep_kernel(q_ref, k_ref, v_ref, *refs):
    x, _, _, _ = place()
    outs, sems = refs[:4], refs[4]
    copies = []
    for s in (1, 2, 3, 0):
        h = lax.rem(x + s, 4)
        start = pl.multiple_of(h * HEAD, HEAD)
        for g in range(GROUP):
            column = pl.multiple_of(h * (GROUP * HEAD) + g * HEAD, HEAD)
            copies.append((q_ref.at[:, pl.ds(column, HEAD)], outs[s].at[pl.ds(g * BLOCK, BLOCK)]))
        copies.append((k_ref.at[:, pl.ds(start, HEAD)], outs[s].at[pl.ds(ROWS, BLOCK)]))
        copies.append((v_ref.at[:, pl.ds(start, HEAD)], outs[s].at[pl.ds(ROWS + BLOCK, BLOCK)]))
    copies = [pltpu.make_async_copy(a, b, sems.at[n]) for n, (a, b) in enumerate(copies)]
    for copy in copies:
        copy.start()
    for copy in copies:
        copy.wait()


def lists_kernel(mask_ref, order_ref, near_ref, far_ref):
    x, y, z, c = place()
    slots = lax.broadcasted_iota(i32, (1, 256), 1)
    order = order_ref[...]

    def slot(x, y, z, c):
        return lax.rem(x, 2) * 128 + z * 16 + y * 4 + lax.div(x, 2) * 2 + c

    def kv_slot(x, y, z, c):
        return (y * 4 + lax.div(x, 2) * 2 + c) * 16 + lax.rem(x, 2) * 8 + z

    i = lax.broadcasted_iota(i32, (16, 1), 0)
    qx = lax.rem(x - lax.rem(i, 4) + 4, 4)
    qy = lax.rem(y - lax.div(i, 4) + 4, 4)
    q_slot = slot(qx, qy, z, c)
    j = lax.broadcasted_iota(i32, (64, 1), 0)
    unit = lax.div(j, 4)
    zs = jnp.zeros_like(unit)
    cs = jnp.zeros_like(unit)
    for n, (k, other) in enumerate(UNITS):
        zs = jnp.where(unit == n, k, zs)
        cs = jnp.where(unit == n, other, cs)
    kc = lax.rem(c + cs, 2)
    k_slot = kv_slot(lax.rem(x - lax.rem(j, 4) + 4, 4), y, lax.rem(z - zs + 8, 8), kc)

    def one_hot(slot_col):
        block = jnp.sum(jnp.where(slots == slot_col, order, 0), axis=1, keepdims=True)
        return jnp.where(slots == block, 1.0, 0.0).astype(bf16)

    q_hot, k_hot = one_hot(q_slot), one_hot(k_slot)
    rows = jnp.dot(q_hot, mask_ref[...].astype(f32).astype(bf16), preferred_element_type=f32)
    contract = (((1,), (1,)), ((), ()))
    opened = lax.dot_general(rows.astype(bf16), k_hot, contract, preferred_element_type=f32)
    same = lax.dot_general(q_hot, k_hot, contract, preferred_element_type=f32)
    off = opened * (1.0 - same)
    first = lax.broadcasted_iota(i32, (64, 64), 0)
    second = lax.broadcasted_iota(i32, (64, 64), 1)
    below = (first < second) & ((first < SPLIT) == (second < SPLIT))
    below = jnp.where(below, 1.0, 0.0).astype(bf16)
    rank = jnp.dot(off.astype(bf16), below, preferred_element_type=f32)
    lane = lax.broadcasted_iota(i32, (16, LANES), 1)
    lanes = lane.astype(f32)
    target = lax.rem(qx, 2) * 8 + qy * 2 + lax.div(qx, 2)
    for ref, low, high in ((near_ref, 0, SPLIT), (far_ref, SPLIT, 64)):
        n_off = jnp.sum(off[:, low:high], axis=1, keepdims=True)
        n_dia = jnp.sum(same[:, low:high], axis=1, keepdims=True)
        pos = jnp.where(same > 0.5, n_off, jnp.where(off > 0.5, rank, 999.0))
        out = jnp.zeros((16, LANES), f32)
        for n in range(low, high):
            out = out + jnp.where(pos[:, n : n + 1] == lanes, float(n - low), 0.0)
        out = jnp.where(lane == CNT, n_off + n_dia, out)
        out = jnp.where(lane == DIA, n_dia, out)
        ref[:16, :] = jnp.where(lane == DST, target, out.astype(i32))
        ref[16:, :] = jnp.zeros((8, LANES), i32)


def attend_kernel(kv_sizes, final, info, *refs):
    n_kv = len(kv_sizes)
    q_in, kv_in, refs = refs[:4], refs[4 : 4 + n_kv], refs[4 + n_kv :]
    if final:
        m_in, l_in, acc_in, o_ref, m_s, l_s, acc_s = refs[:7]
        refs = refs[7:]
    else:
        m_s, l_s, acc_s = refs[:3]
        refs = refs[3:]
    q_s, kv_s, work_q, work_g, sems = refs
    copies = []
    for t in range(4):
        copies.append((q_in[t], q_s.at[pl.ds(t * 4, 4)]))
    for n in range(n_kv):
        copies.append((kv_in[n], kv_s.at[pl.ds(sum(kv_sizes[:n]), kv_sizes[n])]))
    copies = [pltpu.make_async_copy(a, b, sems.at[n]) for n, (a, b) in enumerate(copies)]
    for copy in copies:
        copy.start()

    def fill(qb, t):
        def put(g, t):
            work_q[t] = qb
            work_g[t] = g * TILES
            return t + 1

        return lax.fori_loop(0, jnp.maximum(info[qb, CNT] - 1, 0) // TILES, put, t)

    items = lax.fori_loop(0, 16, fill, 0)
    for u in range(UNROLL - 1):
        work_q[items + u] = 16
        work_g[items + u] = 0
    for copy in copies:
        copy.wait()
    q_s[16] = q_s[0]

    row = lax.broadcasted_iota(i32, (BLOCK, ROWS), 0)
    ahead = row - lax.rem(lax.broadcasted_iota(i32, (BLOCK, ROWS), 1), BLOCK)

    def tiles(qb, base, part):
        rows = pl.ds(part * BLOCK, BLOCK)
        return jnp.concatenate([kv_s[info[qb, base + n], rows, :] for n in range(TILES)], axis=0)

    def scores(qb, base):
        return lax.dot_general(
            tiles(qb, base, 0), q_s[qb], (((1,), (1,)), ((), ())), preferred_element_type=f32
        )

    def weighted(qb, base, p):
        return lax.dot_general(
            tiles(qb, base, 1), p, (((0,), (0,)), ((), ())), preferred_element_type=f32
        )

    def masked(s, qb, base):
        n, dia = info[qb, CNT], info[qb, DIA]
        parts = []
        for i in range(TILES):
            limit = jnp.where(base + i < n - dia, 1000, jnp.where(base + i < n, 0, -1000))
            parts.append(jnp.where(ahead <= limit, s[i * BLOCK : (i + 1) * BLOCK], NEG))
        return jnp.concatenate(parts, axis=0)

    def pipeline(items, weigh, store):
        s, p = scores(*items[0]), None
        for n, item in enumerate(items):
            ahead_s = scores(*items[n + 1]) if n + 1 < len(items) else None
            if p is not None:
                store(items[n - 1][0], weighted(*items[n - 1], p))
            p, s = weigh(s, *item).astype(bf16), ahead_s
        store(items[-1][0], weighted(*items[-1], p))

    def weigh_last(s, qb, base):
        s = masked(s, qb, base)
        m = jnp.max(s, axis=0, keepdims=True) * LOG2E_SCALE
        p = jnp.exp2(s * LOG2E_SCALE - m)
        m_s[qb] = m
        l_s[qb] = jnp.where(info[qb, CNT] > 0, jnp.sum(p, axis=0, keepdims=True), 0.0)
        return p

    def store_last(qb, value):
        acc_s[qb] = value

    def last(t, carry):
        items = []
        for u in range(UNROLL):
            qb = t * UNROLL + u
            items.append((qb, jnp.maximum(info[qb, CNT] - 1, 0) // TILES * TILES))
        pipeline(items, weigh_last, store_last)
        return carry

    lax.fori_loop(0, 16 // UNROLL, last, 0)

    def weigh_full(s, qb, base):
        p = jnp.exp2(s * LOG2E_SCALE - m_s[qb])
        l_s[qb] += jnp.sum(p, axis=0, keepdims=True)
        return p

    def store_full(qb, value):
        acc_s[qb] += value

    def full(t, carry):
        pipeline(
            [(work_q[t * UNROLL + u], work_g[t * UNROLL + u]) for u in range(UNROLL)],
            weigh_full,
            store_full,
        )
        return carry

    m_s[16] = jnp.zeros((1, ROWS), f32)
    lax.fori_loop(0, (items + UNROLL - 1) // UNROLL, full, 0)

    def safe(qb, carry):
        def step(g, state):
            m, l, acc = state
            s = masked(scores(qb, g * TILES), qb, g * TILES)
            m_new = jnp.maximum(m, jnp.max(s, axis=0, keepdims=True) * LOG2E_SCALE)
            p = jnp.exp2(s * LOG2E_SCALE - m_new)
            fade = jnp.exp2(m - m_new)
            l = l * fade + jnp.sum(p, axis=0, keepdims=True)
            return m_new, l, acc * fade + weighted(qb, g * TILES, p.astype(bf16))

        start = (jnp.full((1, ROWS), NEG), jnp.zeros((1, ROWS), f32), jnp.zeros((HEAD, ROWS), f32))
        m_s[qb], l_s[qb], acc_s[qb] = lax.fori_loop(
            0, (info[qb, CNT] + TILES - 1) // TILES, step, start
        )
        return carry

    @pl.when(jnp.logical_not(jnp.max(l_s[:16]) < 1e30))
    def _():
        lax.fori_loop(0, 16, safe, 0)

    if not final:
        return

    def finish(qb):
        l1, l2 = l_in[qb], l_s[qb]
        m1 = jnp.where(l1 > 0, m_in[qb], NEG)
        m2 = jnp.where(l2 > 0, m_s[qb], NEG)
        m = jnp.maximum(m1, m2)
        w1 = jnp.where(l1 > 0, jnp.exp2(m1 - m), 0.0)
        w2 = jnp.where(l2 > 0, jnp.exp2(m2 - m), 0.0)
        l = l1 * w1 + l2 * w2
        some = l > 0
        inverse = jnp.where(some, 1.0 / l, 0.0)
        target = info[qb, DST]
        o = acc_in[qb] * (w1 * inverse) + acc_s[qb] * (w2 * inverse)
        o_ref[target, :HEAD, :] = o.astype(bf16)
        lse = jnp.where(some, m * math.log(2.0) + jnp.log(l), NEG)
        high = lse.astype(bf16).astype(f32)
        mid = (lse - high).astype(bf16).astype(f32)
        low = lse - high - mid
        at = lax.broadcasted_iota(i32, (TAIL, ROWS), 0)
        tail = jnp.where(at == 0, high, jnp.where(at == 1, mid, jnp.where(at == 2, low, 0.0)))
        o_ref[target, HEAD:, :] = tail.astype(bf16)

    def finish_some(t, carry):
        for u in range(4):
            finish(t * 4 + u)
        return carry

    lax.fori_loop(0, 4, finish_some, 0)


def combine_kernel(in_ref, out_ref, lse_ref):
    for h in range(4):
        src = [(h % 2) * 8 + c * 2 + h // 2 for c in range(4)]
        lses = []
        for s in src:
            tail = in_ref[s, HEAD:, :].astype(f32)
            lses.append(tail[0:1] + tail[1:2] + tail[2:3])
        top = jnp.maximum(jnp.maximum(lses[0], lses[1]), jnp.maximum(lses[2], lses[3]))
        weights = [jnp.exp(lse - top) for lse in lses]
        total = weights[0] + weights[1] + weights[2] + weights[3]
        inverse = 1.0 / total
        o = sum(in_ref[s, :HEAD, :].astype(f32) * (w * inverse) for s, w in zip(src, weights))
        o = o.T.astype(bf16)
        lse = top + jnp.log(total)
        for g in range(GROUP):
            rows = slice(g * BLOCK, (g + 1) * BLOCK)
            head = h * GROUP + g
            out_ref[:, head * HEAD : (head + 1) * HEAD] = o[rows]
            lse_ref[head : head + 1, :] = lse[:, rows]


def attend(info, qs, kv, state=()):
    sizes = tuple(a.shape[0] for a in kv)
    blocks, final = sum(sizes), bool(state)
    shapes = [(17, 1, ROWS), (17, 1, ROWS), (17, HEAD, ROWS)]
    out = [jax.ShapeDtypeStruct(shape, f32) for shape in shapes]
    scratch = [
        pltpu.VMEM((17, ROWS, HEAD), bf16),
        pltpu.VMEM((blocks, 2 * BLOCK, HEAD), bf16),
        pltpu.SMEM((4 * blocks + UNROLL,), i32),
        pltpu.SMEM((4 * blocks + UNROLL,), i32),
        pltpu.SemaphoreType.DMA((4 + len(kv),)),
    ]
    if final:
        scratch = [pltpu.VMEM(shape, f32) for shape in shapes] + scratch
        out = jax.ShapeDtypeStruct((16, HEAD + TAIL, ROWS), bf16)
    return call(
        functools.partial(attend_kernel, sizes, final),
        [SMEM] + [ANY] * (4 + len(kv)) + [VMEM] * len(state),
        out,
        VMEM if final else [VMEM] * 3,
        scratch,
        flops=blocks * 200_000_000,
        size=8_000_000,
    )(info, *qs, *kv, *state)


def body(queries, keys, values, tile_mask, slot_order):
    with jax.named_scope("prep"):
        piece = jax.ShapeDtypeStruct((ROWS + 2 * BLOCK, HEAD), bf16)
        pieces = call(
            prep_kernel,
            [pl.BlockSpec(memory_space=pltpu.HBM)] * 3,
            [piece] * 4,
            [VMEM] * 4,
            [pltpu.SemaphoreType.DMA((24,))],
        )(queries, keys, values)
    with jax.named_scope("lists"):
        table = jax.ShapeDtypeStruct((24, LANES), i32)
        near_info, far_info = call(
            lists_kernel, [VMEM, VMEM], [table, table], [VMEM, VMEM]
        )(tile_mask, slot_order.reshape(1, 256))
    with jax.named_scope("heads"):
        pieces = [pieces[0]] + [shift_x(pieces[s], s) for s in (1, 2, 3)]
        pieces, near_info, far_info = lax.optimization_barrier((pieces, near_info, far_info))
        own_kv = jnp.stack([p[ROWS:] for p in pieces])
        own_q = jnp.stack([p[:ROWS] for p in pieces])
    with jax.named_scope("gather"):
        qs = [own_q] + [shift_y(own_q, t) for t in (2, 1, 3)]
        qs[1], qs[2] = qs[2], qs[1]
        kv = {0: own_kv, 1: shift_z(own_kv, 1), 7: shift_z(own_kv, 7)}
        kv[2] = shift_z(kv[1], 1)
        kv[6] = shift_z(kv[7], 7)
        kv, qs = lax.optimization_barrier((kv, qs))
        near = jnp.concatenate([kv[s] for s in NEAR])
        near_swap = swap_core(near)
        kv[3] = shift_z(kv[2], 1)
        kv[5] = shift_z(kv[6], 7)
        kv[4] = shift_z(kv[2], 2)
    with jax.named_scope("near"):
        state = attend(near_info, qs, [near, near_swap])
        far, state = lax.optimization_barrier(([kv[s] for s in FAR], state))
        far = jnp.concatenate(far)
        far_swap = swap_core(far)
    with jax.named_scope("far"):
        partial = attend(far_info, qs, [far, far_swap], state)
    with jax.named_scope("exchange"):
        parts = lax.all_to_all(partial, ("xl", "y", "xh"), split_axis=0, concat_axis=0, tiled=True)
    with jax.named_scope("combine"):
        return call(
            combine_kernel,
            [VMEM],
            [jax.ShapeDtypeStruct((BLOCK, 16 * HEAD), bf16), jax.ShapeDtypeStruct((16, BLOCK), f32)],
            [VMEM, VMEM],
        )(parts)


def solution(mesh):
    fine = Mesh(mesh.devices.reshape(SIZES), AXES)
    by_query, by_key = AXES, ("y", "xh", "core", "xl", "z")
    return jax.shard_map(
        body,
        mesh=fine,
        in_specs=(P(by_query, None), P(by_key, None), P(by_key, None), P(), P()),
        out_specs=(P(by_query, None), P(None, by_query)),
        check_vma=False,
    )
```

```python
import functools
import math

import jax
import jax.numpy as jnp
import numpy as np
from jax import lax
from jax.experimental import pallas as pl
from jax.experimental.pallas import tpu as pltpu
from jax.sharding import Mesh
from jax.sharding import PartitionSpec as P

AXES = ("xl", "z", "y", "xh", "core")
SIZES = (2, 8, 4, 2, 2)
HEAD = 128
BLOCK = 64
GROUP = 4
ROWS = GROUP * BLOCK
SCALE = 1.0 / math.sqrt(HEAD)
LOG2E_SCALE = math.log2(math.e) * SCALE
NEG = -1e30
LANES = 128
CNT, DIA, DST = 120, 121, 122
TAIL = 16
TILES = 8
FIN = 4
LASTU = 16
UNROLL = 16
Z_ORDER = (0, 1, 7, 2, 6, 3, 5, 4)
UNITS = [(k, c) for c in (0, 1) for k in Z_ORDER]

VMEM = pl.BlockSpec(memory_space=pltpu.VMEM)
SMEM = pl.BlockSpec(memory_space=pltpu.SMEM)
ANY = pl.BlockSpec(memory_space=pl.ANY)
f32, bf16, i32 = jnp.float32, jnp.bfloat16, jnp.int32


def permute(array, move):
    pairs = []
    for i in range(256):
        xl, z, y, xh, c = (int(v) for v in np.unravel_index(i, SIZES))
        x, y, z, c = move(2 * xh + xl, y, z, c)
        pairs.append((i, int(np.ravel_multi_index((x % 2, z, y, x // 2, c), SIZES))))
    return lax.ppermute(array, AXES, pairs)


def shift_x(array, k):
    return permute(array, lambda x, y, z, c: ((x + k) % 4, y, z, c))


def shift_y(array, k):
    return permute(array, lambda x, y, z, c: (x, (y + k) % 4, z, c))


def shift_z(array, k):
    return permute(array, lambda x, y, z, c: (x, y, (z + k) % 8, c))


def swap_core(array):
    return permute(array, lambda x, y, z, c: (x, y, z, 1 - c))


def call(kernel, in_specs, out_shape, out_specs, scratch=(), flops=0, size=0, limit=48):
    return pl.pallas_call(
        kernel,
        in_specs=in_specs,
        out_specs=out_specs,
        out_shape=out_shape,
        scratch_shapes=scratch,
        cost_estimate=pl.CostEstimate(flops=flops, bytes_accessed=size, transcendentals=0),
        compiler_params=pltpu.CompilerParams(vmem_limit_bytes=limit << 20),
    )


def place():
    x = 2 * lax.axis_index("xh") + lax.axis_index("xl")
    return x, lax.axis_index("y"), lax.axis_index("z"), lax.axis_index("core")


def prep_kernel(q_ref, k_ref, v_ref, *refs):
    x, _, _, _ = place()
    outs, sems = refs[:4], refs[4]
    copies = []
    for s in (1, 2, 3, 0):
        h = lax.rem(x + s, 4)
        start = pl.multiple_of(h * HEAD, HEAD)
        for g in range(GROUP):
            column = pl.multiple_of(h * (GROUP * HEAD) + g * HEAD, HEAD)
            copies.append((q_ref.at[:, pl.ds(column, HEAD)], outs[s].at[pl.ds(g * BLOCK, BLOCK)]))
        copies.append((k_ref.at[:, pl.ds(start, HEAD)], outs[s].at[pl.ds(ROWS, BLOCK)]))
        copies.append((v_ref.at[:, pl.ds(start, HEAD)], outs[s].at[pl.ds(ROWS + BLOCK, BLOCK)]))
    copies = [pltpu.make_async_copy(a, b, sems.at[n]) for n, (a, b) in enumerate(copies)]
    for copy in copies:
        copy.start()
    for copy in copies:
        copy.wait()


def lists_kernel(mask_ref, order_ref, info_ref):
    x, y, z, c = place()
    slots = lax.broadcasted_iota(i32, (1, 256), 1)
    order = order_ref[...]

    def slot(x, y, z, c):
        return lax.rem(x, 2) * 128 + z * 16 + y * 4 + lax.div(x, 2) * 2 + c

    def kv_slot(x, y, z, c):
        return (y * 4 + lax.div(x, 2) * 2 + c) * 16 + lax.rem(x, 2) * 8 + z

    i = lax.broadcasted_iota(i32, (16, 1), 0)
    qx = lax.rem(x - lax.rem(i, 4) + 4, 4)
    qy = lax.rem(y - lax.div(i, 4) + 4, 4)
    q_slot = slot(qx, qy, z, c)
    j = lax.broadcasted_iota(i32, (64, 1), 0)
    unit = lax.div(j, 4)
    zs = jnp.zeros_like(unit)
    cs = jnp.zeros_like(unit)
    for n, (k, other) in enumerate(UNITS):
        zs = jnp.where(unit == n, k, zs)
        cs = jnp.where(unit == n, other, cs)
    kc = lax.rem(c + cs, 2)
    k_slot = kv_slot(lax.rem(x - lax.rem(j, 4) + 4, 4), y, lax.rem(z - zs + 8, 8), kc)

    def one_hot(slot_col):
        block = jnp.sum(jnp.where(slots == slot_col, order, 0), axis=1, keepdims=True)
        return jnp.where(slots == block, 1.0, 0.0).astype(bf16)

    q_hot, k_hot = one_hot(q_slot), one_hot(k_slot)
    rows = jnp.dot(q_hot, mask_ref[...].astype(f32).astype(bf16), preferred_element_type=f32)
    contract = (((1,), (1,)), ((), ()))
    opened = lax.dot_general(rows.astype(bf16), k_hot, contract, preferred_element_type=f32)
    same = lax.dot_general(q_hot, k_hot, contract, preferred_element_type=f32)
    off = opened * (1.0 - same)
    first = lax.broadcasted_iota(i32, (64, 64), 0)
    second = lax.broadcasted_iota(i32, (64, 64), 1)
    below = jnp.where(first < second, 1.0, 0.0).astype(bf16)
    rank = jnp.dot(off.astype(bf16), below, preferred_element_type=f32)
    lane = lax.broadcasted_iota(i32, (16, LANES), 1)
    lanes = lane.astype(f32)
    target = lax.rem(qx, 2) * 8 + qy * 2 + lax.div(qx, 2)
    for ref, low, high in ((info_ref, 0, 64),):
        n_off = jnp.sum(off[:, low:high], axis=1, keepdims=True)
        n_dia = jnp.sum(same[:, low:high], axis=1, keepdims=True)
        pos = jnp.where(same > 0.5, n_off, jnp.where(off > 0.5, rank, 999.0))
        out = jnp.zeros((16, LANES), f32)
        for n in range(low, high):
            out = out + jnp.where(pos[:, n : n + 1] == lanes, float(n - low), 0.0)
        out = jnp.where(lane == CNT, n_off + n_dia, out)
        out = jnp.where(lane == DIA, n_dia, out)
        ref[:16, :] = jnp.where(lane == DST, target, out.astype(i32))
        ref[16:, :] = jnp.zeros((8, LANES), i32)


def attend_kernel(kv_sizes, info, *refs):
    n_kv = len(kv_sizes)
    q_in, kv_in, refs = refs[:4], refs[4 : 4 + n_kv], refs[4 + n_kv :]
    o_ref, m_s, l_s, acc_s, q_s, kv_s, work_q, work_g, sems = refs
    copies = [(q_in[t], q_s.at[pl.ds(t * 4, 4)]) for t in range(4)]
    for n in range(n_kv):
        copies.append((kv_in[n], kv_s.at[pl.ds(sum(kv_sizes[:n]), kv_sizes[n])]))
    copies = [pltpu.make_async_copy(a, b, sems.at[n]) for n, (a, b) in enumerate(copies)]
    for copy in copies:
        copy.start()

    def fill(qb, t):
        def put(g, t):
            work_q[t] = qb
            work_g[t] = g * TILES
            return t + 1

        return lax.fori_loop(0, jnp.maximum(info[qb, CNT] - 1, 0) // TILES, put, t)

    items = lax.fori_loop(0, 16, fill, 0)
    for u in range(UNROLL - 1):
        work_q[items + u] = 16
        work_g[items + u] = 0
    for copy in copies:
        copy.wait()
    q_s[16] = q_s[0]

    row = lax.broadcasted_iota(i32, (BLOCK, ROWS), 0)
    ahead = row - lax.rem(lax.broadcasted_iota(i32, (BLOCK, ROWS), 1), BLOCK)

    def tiles(qb, base, part):
        rows = pl.ds(part * BLOCK, BLOCK)
        return jnp.concatenate([kv_s[info[qb, base + n], rows, :] for n in range(TILES)], axis=0)

    def scores(qb, base):
        return lax.dot_general(
            tiles(qb, base, 0), q_s[qb], (((1,), (1,)), ((), ())), preferred_element_type=f32
        )

    def weighted(qb, base, p):
        return lax.dot_general(
            tiles(qb, base, 1), p, (((0,), (0,)), ((), ())), preferred_element_type=f32
        )

    def masked(s, qb, base):
        n, dia = info[qb, CNT], info[qb, DIA]
        parts = []
        for i in range(TILES):
            limit = jnp.where(base + i < n - dia, 1000, jnp.where(base + i < n, 0, -1000))
            parts.append(jnp.where(ahead <= limit, s[i * BLOCK : (i + 1) * BLOCK], NEG))
        return jnp.concatenate(parts, axis=0)

    def pipeline(items, weigh, store):
        s, p = scores(*items[0]), None
        for n, item in enumerate(items):
            ahead_s = scores(*items[n + 1]) if n + 1 < len(items) else None
            if p is not None:
                store(items[n - 1][0], weighted(*items[n - 1], p))
            p, s = weigh(s, *item).astype(bf16), ahead_s
        store(items[-1][0], weighted(*items[-1], p))

    def weigh_last(s, qb, base):
        s = masked(s, qb, base)
        m = jnp.max(s, axis=0, keepdims=True) * LOG2E_SCALE
        p = jnp.exp2(s * LOG2E_SCALE - m)
        m_s[qb] = m
        l_s[qb] = jnp.where(info[qb, CNT] > 0, jnp.sum(p, axis=0, keepdims=True), 0.0)
        return p

    def store_last(qb, value):
        acc_s[qb] = value

    def last(t, carry):
        items = []
        for u in range(LASTU):
            qb = t * LASTU + u
            items.append((qb, jnp.maximum(info[qb, CNT] - 1, 0) // TILES * TILES))
        pipeline(items, weigh_last, store_last)
        return carry

    lax.fori_loop(0, 16 // LASTU, last, 0)

    def weigh_full(s, qb, base):
        p = jnp.exp2(s * LOG2E_SCALE - m_s[qb])
        l_s[qb] += jnp.sum(p, axis=0, keepdims=True)
        return p

    def store_full(qb, value):
        acc_s[qb] += value

    def full(t, carry):
        pipeline(
            [(work_q[t * UNROLL + u], work_g[t * UNROLL + u]) for u in range(UNROLL)],
            weigh_full,
            store_full,
        )
        return carry

    m_s[16] = jnp.zeros((1, ROWS), f32)
    lax.fori_loop(0, (items + UNROLL - 1) // UNROLL, full, 0)

    def safe(qb, carry):
        def step(g, state):
            m, l, acc = state
            s = masked(scores(qb, g * TILES), qb, g * TILES)
            m_new = jnp.maximum(m, jnp.max(s, axis=0, keepdims=True) * LOG2E_SCALE)
            p = jnp.exp2(s * LOG2E_SCALE - m_new)
            fade = jnp.exp2(m - m_new)
            l = l * fade + jnp.sum(p, axis=0, keepdims=True)
            return m_new, l, acc * fade + weighted(qb, g * TILES, p.astype(bf16))

        start = (jnp.full((1, ROWS), NEG), jnp.zeros((1, ROWS), f32), jnp.zeros((HEAD, ROWS), f32))
        m_s[qb], l_s[qb], acc_s[qb] = lax.fori_loop(
            0, (info[qb, CNT] + TILES - 1) // TILES, step, start
        )
        return carry

    @pl.when(jnp.logical_not(jnp.max(l_s[:16]) < 1e30))
    def _():
        lax.fori_loop(0, 16, safe, 0)

    def finish(qb):
        l = l_s[qb]
        some = l > 0
        inverse = jnp.where(some, 1.0 / l, 0.0)
        target = info[qb, DST]
        o_ref[target, :HEAD, :] = (acc_s[qb] * inverse).astype(bf16)
        lse = jnp.where(some, m_s[qb] * math.log(2.0) + jnp.log(l), NEG)
        high = lse.astype(bf16).astype(f32)
        mid = (lse - high).astype(bf16).astype(f32)
        low = lse - high - mid
        at = lax.broadcasted_iota(i32, (TAIL, ROWS), 0)
        tail = jnp.where(at == 0, high, jnp.where(at == 1, mid, jnp.where(at == 2, low, 0.0)))
        o_ref[target, HEAD:, :] = tail.astype(bf16)

    def finish_some(t, carry):
        for u in range(FIN):
            finish(t * FIN + u)
        return carry

    lax.fori_loop(0, 16 // FIN, finish_some, 0)


def combine_kernel(in_ref, out_ref, lse_ref):
    for h in range(4):
        src = [(h % 2) * 8 + c * 2 + h // 2 for c in range(4)]
        lses = []
        for s in src:
            tail = in_ref[s, HEAD:, :].astype(f32)
            lses.append(tail[0:1] + tail[1:2] + tail[2:3])
        top = jnp.maximum(jnp.maximum(lses[0], lses[1]), jnp.maximum(lses[2], lses[3]))
        weights = [jnp.exp(lse - top) for lse in lses]
        total = weights[0] + weights[1] + weights[2] + weights[3]
        inverse = 1.0 / total
        o = sum(in_ref[s, :HEAD, :].astype(f32) * (w * inverse) for s, w in zip(src, weights))
        o = o.T.astype(bf16)
        lse = top + jnp.log(total)
        for g in range(GROUP):
            rows = slice(g * BLOCK, (g + 1) * BLOCK)
            head = h * GROUP + g
            out_ref[:, head * HEAD : (head + 1) * HEAD] = o[rows]
            lse_ref[head : head + 1, :] = lse[:, rows]


def attend(info, qs, kv):
    sizes = tuple(a.shape[0] for a in kv)
    blocks = sum(sizes)
    return call(
        functools.partial(attend_kernel, sizes),
        [SMEM] + [ANY] * (4 + len(kv)),
        jax.ShapeDtypeStruct((16, HEAD + TAIL, ROWS), bf16),
        VMEM,
        [
            pltpu.VMEM((17, 1, ROWS), f32),
            pltpu.VMEM((17, 1, ROWS), f32),
            pltpu.VMEM((17, HEAD, ROWS), f32),
            pltpu.VMEM((17, ROWS, HEAD), bf16),
            pltpu.VMEM((blocks, 2 * BLOCK, HEAD), bf16),
            pltpu.SMEM((4 * blocks + UNROLL,), i32),
            pltpu.SMEM((4 * blocks + UNROLL,), i32),
            pltpu.SemaphoreType.DMA((4 + len(kv),)),
        ],
        flops=blocks * 200_000_000,
        size=8_000_000,
    )(info, *qs, *kv)


def body(queries, keys, values, tile_mask, slot_order):
    with jax.named_scope("prep"):
        piece = jax.ShapeDtypeStruct((ROWS + 2 * BLOCK, HEAD), bf16)
        pieces = call(
            prep_kernel,
            [pl.BlockSpec(memory_space=pltpu.HBM)] * 3,
            [piece] * 4,
            [VMEM] * 4,
            [pltpu.SemaphoreType.DMA((24,))],
        )(queries, keys, values)
    with jax.named_scope("lists"):
        table = jax.ShapeDtypeStruct((24, LANES), i32)
        info = call(lists_kernel, [VMEM, VMEM], table, VMEM)(tile_mask, slot_order.reshape(1, 256))
    with jax.named_scope("heads"):
        pieces = [pieces[0]] + [shift_x(pieces[s], s) for s in (1, 2, 3)]
        pieces, info = lax.optimization_barrier((pieces, info))
        own_kv = jnp.stack([p[ROWS:] for p in pieces])
        own_q = jnp.stack([p[:ROWS] for p in pieces])
    with jax.named_scope("gather"):
        qs = [own_q] + [shift_y(own_q, t) for t in (1, 2, 3)]
        kv = {0: own_kv, 1: shift_z(own_kv, 1), 7: shift_z(own_kv, 7)}
        kv[2] = shift_z(kv[1], 1)
        kv[6] = shift_z(kv[7], 7)
        kv[3] = shift_z(kv[2], 1)
        kv[5] = shift_z(kv[6], 7)
        kv[4] = shift_z(kv[2], 2)
        kv, qs = lax.optimization_barrier((kv, qs))
        own = jnp.concatenate([kv[s] for s in Z_ORDER])
        other = swap_core(own)
    with jax.named_scope("attend"):
        partial = attend(info, qs, [own, other])
    with jax.named_scope("exchange"):
        parts = lax.all_to_all(partial, ("xl", "y", "xh"), split_axis=0, concat_axis=0, tiled=True)
    with jax.named_scope("combine"):
        return call(
            combine_kernel,
            [VMEM],
            [jax.ShapeDtypeStruct((BLOCK, 16 * HEAD), bf16), jax.ShapeDtypeStruct((16, BLOCK), f32)],
            [VMEM, VMEM],
        )(parts)


def solution(mesh):
    fine = Mesh(mesh.devices.reshape(SIZES), AXES)
    by_query, by_key = AXES, ("y", "xh", "core", "xl", "z")
    return jax.shard_map(
        body,
        mesh=fine,
        in_specs=(P(by_query, None), P(by_key, None), P(by_key, None), P(), P()),
        out_specs=(P(by_query, None), P(None, by_query)),
        check_vma=False,
    )
```

```python
import functools
import math

import jax
import jax.numpy as jnp
import numpy as np
from jax import lax
from jax.experimental import pallas as pl
from jax.experimental.pallas import tpu as pltpu
from jax.sharding import Mesh
from jax.sharding import PartitionSpec as P

AXES = ("xl", "z", "y", "xh", "core")
SIZES = (2, 8, 4, 2, 2)
HEAD = 128
BLOCK = 64
GROUP = 4
ROWS = GROUP * BLOCK
SCALE = 1.0 / math.sqrt(HEAD)
LOG2E_SCALE = math.log2(math.e) * SCALE
NEG = -1e30
LANES = 128
CNT, DIA, DST = 120, 121, 122
TAIL = 16
TILES = 8
FIN = 4
LASTU = 16
UNROLL = 16
Z_ORDER = (0, 1, 7, 2, 6, 3, 5, 4)
UNITS = [(k, c) for c in (0, 1) for k in Z_ORDER]

VMEM = pl.BlockSpec(memory_space=pltpu.VMEM)
SMEM = pl.BlockSpec(memory_space=pltpu.SMEM)
ANY = pl.BlockSpec(memory_space=pl.ANY)
f32, bf16, i32 = jnp.float32, jnp.bfloat16, jnp.int32


def permute(array, move):
    pairs = []
    for i in range(256):
        xl, z, y, xh, c = (int(v) for v in np.unravel_index(i, SIZES))
        x, y, z, c = move(2 * xh + xl, y, z, c)
        pairs.append((i, int(np.ravel_multi_index((x % 2, z, y, x // 2, c), SIZES))))
    return lax.ppermute(array, AXES, pairs)


def shift_x(array, k):
    return permute(array, lambda x, y, z, c: ((x + k) % 4, y, z, c))


def shift_y(array, k):
    return permute(array, lambda x, y, z, c: (x, (y + k) % 4, z, c))


def shift_z(array, k):
    return permute(array, lambda x, y, z, c: (x, y, (z + k) % 8, c))


def swap_core(array):
    return permute(array, lambda x, y, z, c: (x, y, z, 1 - c))


def call(kernel, in_specs, out_shape, out_specs, scratch=(), flops=0, size=0, limit=48):
    return pl.pallas_call(
        kernel,
        in_specs=in_specs,
        out_specs=out_specs,
        out_shape=out_shape,
        scratch_shapes=scratch,
        cost_estimate=pl.CostEstimate(flops=flops, bytes_accessed=size, transcendentals=0),
        compiler_params=pltpu.CompilerParams(vmem_limit_bytes=limit << 20),
    )


def place():
    x = 2 * lax.axis_index("xh") + lax.axis_index("xl")
    return x, lax.axis_index("y"), lax.axis_index("z"), lax.axis_index("core")


def prep_kernel(q_ref, k_ref, v_ref, *refs):
    x, _, _, _ = place()
    outs, sems = refs[:4], refs[4]
    copies = []
    for s in (1, 2, 3, 0):
        h = lax.rem(x + s, 4)
        start = pl.multiple_of(h * HEAD, HEAD)
        for g in range(GROUP):
            column = pl.multiple_of(h * (GROUP * HEAD) + g * HEAD, HEAD)
            copies.append((q_ref.at[:, pl.ds(column, HEAD)], outs[s].at[pl.ds(g * BLOCK, BLOCK)]))
        copies.append((k_ref.at[:, pl.ds(start, HEAD)], outs[s].at[pl.ds(ROWS, BLOCK)]))
        copies.append((v_ref.at[:, pl.ds(start, HEAD)], outs[s].at[pl.ds(ROWS + BLOCK, BLOCK)]))
    copies = [pltpu.make_async_copy(a, b, sems.at[n]) for n, (a, b) in enumerate(copies)]
    for copy in copies:
        copy.start()
    for copy in copies:
        copy.wait()


def lists_kernel(mask_ref, order_ref, info_ref):
    x, y, z, c = place()
    slots = lax.broadcasted_iota(i32, (1, 256), 1)
    order = order_ref[...]

    def slot(x, y, z, c):
        return lax.rem(x, 2) * 128 + z * 16 + y * 4 + lax.div(x, 2) * 2 + c

    def kv_slot(x, y, z, c):
        return (y * 4 + lax.div(x, 2) * 2 + c) * 16 + lax.rem(x, 2) * 8 + z

    i = lax.broadcasted_iota(i32, (16, 1), 0)
    qx = lax.rem(x - lax.rem(i, 4) + 4, 4)
    qy = lax.rem(y - lax.div(i, 4) + 4, 4)
    q_slot = slot(qx, qy, z, c)
    j = lax.broadcasted_iota(i32, (64, 1), 0)
    unit = lax.div(j, 4)
    zs = jnp.zeros_like(unit)
    cs = jnp.zeros_like(unit)
    for n, (k, other) in enumerate(UNITS):
        zs = jnp.where(unit == n, k, zs)
        cs = jnp.where(unit == n, other, cs)
    kc = lax.rem(c + cs, 2)
    k_slot = kv_slot(lax.rem(x - lax.rem(j, 4) + 4, 4), y, lax.rem(z - zs + 8, 8), kc)

    def one_hot(slot_col):
        block = jnp.sum(jnp.where(slots == slot_col, order, 0), axis=1, keepdims=True)
        return jnp.where(slots == block, 1.0, 0.0).astype(bf16)

    q_hot, k_hot = one_hot(q_slot), one_hot(k_slot)
    rows = jnp.dot(q_hot, mask_ref[...].astype(f32).astype(bf16), preferred_element_type=f32)
    contract = (((1,), (1,)), ((), ()))
    opened = lax.dot_general(rows.astype(bf16), k_hot, contract, preferred_element_type=f32)
    same = lax.dot_general(q_hot, k_hot, contract, preferred_element_type=f32)
    off = opened * (1.0 - same)
    first = lax.broadcasted_iota(i32, (64, 64), 0)
    second = lax.broadcasted_iota(i32, (64, 64), 1)
    below = jnp.where(first < second, 1.0, 0.0).astype(bf16)
    rank = jnp.dot(off.astype(bf16), below, preferred_element_type=f32)
    lane = lax.broadcasted_iota(i32, (16, LANES), 1)
    lanes = lane.astype(f32)
    target = qy * 4 + lax.rem(qx, 2) * 2 + lax.div(qx, 2)
    for ref, low, high in ((info_ref, 0, 64),):
        n_off = jnp.sum(off[:, low:high], axis=1, keepdims=True)
        n_dia = jnp.sum(same[:, low:high], axis=1, keepdims=True)
        pos = jnp.where(same > 0.5, n_off, jnp.where(off > 0.5, rank, 999.0))
        out = jnp.zeros((16, LANES), f32)
        for n in range(low, high):
            out = out + jnp.where(pos[:, n : n + 1] == lanes, float(n - low), 0.0)
        out = jnp.where(lane == CNT, n_off + n_dia, out)
        out = jnp.where(lane == DIA, n_dia, out)
        ref[:16, :] = jnp.where(lane == DST, target, out.astype(i32))
        ref[16:, :] = jnp.zeros((8, LANES), i32)


def attend_kernel(kv_sizes, info, *refs):
    n_kv = len(kv_sizes)
    q_in, kv_in, refs = refs[:4], refs[4 : 4 + n_kv], refs[4 + n_kv :]
    o_ref, m_s, l_s, acc_s, q_s, kv_s, work_q, work_g, sems = refs
    copies = [(q_in[t], q_s.at[pl.ds(t * 4, 4)]) for t in range(4)]
    for n in range(n_kv):
        copies.append((kv_in[n], kv_s.at[pl.ds(sum(kv_sizes[:n]), kv_sizes[n])]))
    copies = [pltpu.make_async_copy(a, b, sems.at[n]) for n, (a, b) in enumerate(copies)]
    for copy in copies:
        copy.start()

    def fill(qb, t):
        def put(g, t):
            work_q[t] = qb
            work_g[t] = g * TILES
            return t + 1

        return lax.fori_loop(0, jnp.maximum(info[qb, CNT] - 1, 0) // TILES, put, t)

    items = lax.fori_loop(0, 16, fill, 0)
    for u in range(UNROLL - 1):
        work_q[items + u] = 16
        work_g[items + u] = 0
    for copy in copies:
        copy.wait()
    q_s[16] = q_s[0]

    row = lax.broadcasted_iota(i32, (BLOCK, ROWS), 0)
    ahead = row - lax.rem(lax.broadcasted_iota(i32, (BLOCK, ROWS), 1), BLOCK)

    def tiles(qb, base, part):
        rows = pl.ds(part * BLOCK, BLOCK)
        return jnp.concatenate([kv_s[info[qb, base + n], rows, :] for n in range(TILES)], axis=0)

    def scores(qb, base):
        return lax.dot_general(
            tiles(qb, base, 0), q_s[qb], (((1,), (1,)), ((), ())), preferred_element_type=f32
        )

    def weighted(qb, base, p):
        return lax.dot_general(
            tiles(qb, base, 1), p, (((0,), (0,)), ((), ())), preferred_element_type=f32
        )

    def masked(s, qb, base):
        n, dia = info[qb, CNT], info[qb, DIA]
        parts = []
        for i in range(TILES):
            limit = jnp.where(base + i < n - dia, 1000, jnp.where(base + i < n, 0, -1000))
            parts.append(jnp.where(ahead <= limit, s[i * BLOCK : (i + 1) * BLOCK], NEG))
        return jnp.concatenate(parts, axis=0)

    def pipeline(items, weigh, store):
        s, p = scores(*items[0]), None
        for n, item in enumerate(items):
            ahead_s = scores(*items[n + 1]) if n + 1 < len(items) else None
            if p is not None:
                store(items[n - 1][0], weighted(*items[n - 1], p))
            p, s = weigh(s, *item).astype(bf16), ahead_s
        store(items[-1][0], weighted(*items[-1], p))

    def weigh_last(s, qb, base):
        s = masked(s, qb, base)
        m = jnp.max(s, axis=0, keepdims=True) * LOG2E_SCALE
        p = jnp.exp2(s * LOG2E_SCALE - m)
        m_s[qb] = m
        l_s[qb] = jnp.where(info[qb, CNT] > 0, jnp.sum(p, axis=0, keepdims=True), 0.0)
        return p

    def store_last(qb, value):
        acc_s[qb] = value

    def last(t, carry):
        items = []
        for u in range(LASTU):
            qb = t * LASTU + u
            items.append((qb, jnp.maximum(info[qb, CNT] - 1, 0) // TILES * TILES))
        pipeline(items, weigh_last, store_last)
        return carry

    lax.fori_loop(0, 16 // LASTU, last, 0)

    def weigh_full(s, qb, base):
        p = jnp.exp2(s * LOG2E_SCALE - m_s[qb])
        l_s[qb] += jnp.sum(p, axis=0, keepdims=True)
        return p

    def store_full(qb, value):
        acc_s[qb] += value

    def full(start, count):
        items = [(work_q[start + u], work_g[start + u]) for u in range(count)]
        pipeline(items, weigh_full, store_full)

    def full_step(t, carry):
        full(t * UNROLL, UNROLL)
        return carry

    m_s[16] = jnp.zeros((1, ROWS), f32)
    steps = (items + UNROLL // 2 - 1) // UNROLL
    lax.fori_loop(0, steps, full_step, 0)

    @pl.when(items > steps * UNROLL)
    def _():
        full(steps * UNROLL, UNROLL // 2)


    def safe(qb, carry):
        def step(g, state):
            m, l, acc = state
            s = masked(scores(qb, g * TILES), qb, g * TILES)
            m_new = jnp.maximum(m, jnp.max(s, axis=0, keepdims=True) * LOG2E_SCALE)
            p = jnp.exp2(s * LOG2E_SCALE - m_new)
            fade = jnp.exp2(m - m_new)
            l = l * fade + jnp.sum(p, axis=0, keepdims=True)
            return m_new, l, acc * fade + weighted(qb, g * TILES, p.astype(bf16))

        start = (jnp.full((1, ROWS), NEG), jnp.zeros((1, ROWS), f32), jnp.zeros((HEAD, ROWS), f32))
        m_s[qb], l_s[qb], acc_s[qb] = lax.fori_loop(
            0, (info[qb, CNT] + TILES - 1) // TILES, step, start
        )
        return carry

    @pl.when(jnp.logical_not(jnp.max(l_s[:16]) < 1e30))
    def _():
        lax.fori_loop(0, 16, safe, 0)

    def finish(qb):
        l = l_s[qb]
        some = l > 0
        inverse = jnp.where(some, 1.0 / l, 0.0)
        target = info[qb, DST]
        o = (acc_s[qb] * inverse).astype(bf16)
        lse = jnp.where(some, m_s[qb] * math.log(2.0) + jnp.log(l), NEG)
        high = lse.astype(bf16).astype(f32)
        mid = (lse - high).astype(bf16).astype(f32)
        low = lse - high - mid
        at = lax.broadcasted_iota(i32, (TAIL, LANES), 0)
        tail = jnp.zeros((TAIL, LANES), f32)
        for side in range(2):
            lanes = slice(side * LANES, (side + 1) * LANES)
            o_ref[target, side * HEAD : (side + 1) * HEAD, :] = o[:, lanes]
            for n, term in enumerate((high, mid, low)):
                tail = jnp.where(at == 2 * n + side, term[:, lanes], tail)
        o_ref[target, 2 * HEAD :, :] = tail.astype(bf16)

    def finish_some(t, carry):
        for u in range(FIN):
            finish(t * FIN + u)
        return carry

    lax.fori_loop(0, 16 // FIN, finish_some, 0)


def combine_kernel(in_ref, out_ref, lse_ref):
    for h in range(4):
        src = [c * 4 + (h % 2) * 2 + h // 2 for c in range(4)]
        for side in range(2):
            lses = []
            for s in src:
                tail = in_ref[s, 2 * HEAD :, :].astype(f32)
                lses.append(sum(tail[2 * n + side : 2 * n + side + 1] for n in range(3)))
            top = jnp.maximum(jnp.maximum(lses[0], lses[1]), jnp.maximum(lses[2], lses[3]))
            weights = [jnp.exp(lse - top) for lse in lses]
            total = weights[0] + weights[1] + weights[2] + weights[3]
            inverse = 1.0 / total
            rows = slice(side * HEAD, (side + 1) * HEAD)
            o = sum(in_ref[s, rows, :].astype(f32) * (w * inverse) for s, w in zip(src, weights))
            o = o.T.astype(bf16)
            lse = top + jnp.log(total)
            for g in range(2):
                part = slice(g * BLOCK, (g + 1) * BLOCK)
                head = h * GROUP + side * 2 + g
                out_ref[:, head * HEAD : (head + 1) * HEAD] = o[part]
                lse_ref[head : head + 1, :] = lse[:, part]


def attend(info, qs, kv):
    sizes = tuple(a.shape[0] for a in kv)
    blocks = sum(sizes)
    return call(
        functools.partial(attend_kernel, sizes),
        [SMEM] + [ANY] * (4 + len(kv)),
        jax.ShapeDtypeStruct((16, 2 * HEAD + TAIL, LANES), bf16),
        VMEM,
        [
            pltpu.VMEM((17, 1, ROWS), f32),
            pltpu.VMEM((17, 1, ROWS), f32),
            pltpu.VMEM((17, HEAD, ROWS), f32),
            pltpu.VMEM((17, ROWS, HEAD), bf16),
            pltpu.VMEM((blocks, 2 * BLOCK, HEAD), bf16),
            pltpu.SMEM((4 * blocks + UNROLL,), i32),
            pltpu.SMEM((4 * blocks + UNROLL,), i32),
            pltpu.SemaphoreType.DMA((4 + len(kv),)),
        ],
        flops=blocks * 200_000_000,
        size=8_000_000,
    )(info, *qs, *kv)


def body(queries, keys, values, tile_mask, slot_order):
    with jax.named_scope("prep"):
        piece = jax.ShapeDtypeStruct((ROWS + 2 * BLOCK, HEAD), bf16)
        pieces = call(
            prep_kernel,
            [pl.BlockSpec(memory_space=pltpu.HBM)] * 3,
            [piece] * 4,
            [VMEM] * 4,
            [pltpu.SemaphoreType.DMA((24,))],
        )(queries, keys, values)
    with jax.named_scope("lists"):
        table = jax.ShapeDtypeStruct((24, LANES), i32)
        info = call(lists_kernel, [VMEM, VMEM], table, VMEM)(tile_mask, slot_order.reshape(1, 256))
    with jax.named_scope("heads"):
        pieces = [pieces[0]] + [shift_x(pieces[s], s) for s in (1, 2, 3)]
        pieces, info = lax.optimization_barrier((pieces, info))
        own_kv = jnp.stack([p[ROWS:] for p in pieces])
        own_q = jnp.stack([p[:ROWS] for p in pieces])
    with jax.named_scope("gather"):
        qs = [own_q] + [shift_y(own_q, t) for t in (1, 2, 3)]
        kv = {0: own_kv, 1: shift_z(own_kv, 1), 7: shift_z(own_kv, 7)}
        kv[2] = shift_z(kv[1], 1)
        kv[6] = shift_z(kv[7], 7)
        kv[3] = shift_z(kv[2], 1)
        kv[5] = shift_z(kv[6], 7)
        kv[4] = shift_z(kv[2], 2)
        kv, qs = lax.optimization_barrier((kv, qs))
        own = jnp.concatenate([kv[s] for s in Z_ORDER])
        other = swap_core(own)
    with jax.named_scope("attend"):
        partial = attend(info, qs, [own, other])
    with jax.named_scope("exchange"):
        parts = lax.all_to_all(partial, ("y", "xl", "xh"), split_axis=0, concat_axis=0, tiled=True)
    with jax.named_scope("combine"):
        return call(
            combine_kernel,
            [VMEM],
            [jax.ShapeDtypeStruct((BLOCK, 16 * HEAD), bf16), jax.ShapeDtypeStruct((16, BLOCK), f32)],
            [VMEM, VMEM],
        )(parts)


def solution(mesh):
    fine = Mesh(mesh.devices.reshape(SIZES), AXES)
    by_query, by_key = AXES, ("y", "xh", "core", "xl", "z")
    return jax.shard_map(
        body,
        mesh=fine,
        in_specs=(P(by_query, None), P(by_key, None), P(by_key, None), P(), P()),
        out_specs=(P(by_query, None), P(None, by_query)),
        check_vma=False,
    )
```

```python
import functools
import math

import jax
import jax.numpy as jnp
import numpy as np
from jax import lax
from jax.experimental import pallas as pl
from jax.experimental.pallas import tpu as pltpu
from jax.sharding import Mesh
from jax.sharding import PartitionSpec as P

AXES = ("xl", "z", "y", "xh", "core")
SIZES = (2, 8, 4, 2, 2)
HEAD = 128
BLOCK = 64
GROUP = 4
ROWS = GROUP * BLOCK
SCALE = 1.0 / math.sqrt(HEAD)
LOG2E_SCALE = math.log2(math.e) * SCALE
NEG = -1e30
LANES = 128
CNT, DIA, DST = 120, 121, 122
TAIL = 16
TILES = 8
HALF = 4
HALF_UNROLL = 8
FIN = 4
LASTU = 16
UNROLL = 16
Z_ORDER = (0, 1, 7, 2, 6, 3, 5, 4)
UNITS = [(k, c) for c in (0, 1) for k in Z_ORDER]

VMEM = pl.BlockSpec(memory_space=pltpu.VMEM)
SMEM = pl.BlockSpec(memory_space=pltpu.SMEM)
ANY = pl.BlockSpec(memory_space=pl.ANY)
f32, bf16, i32 = jnp.float32, jnp.bfloat16, jnp.int32


def permute(array, move):
    pairs = []
    for i in range(256):
        xl, z, y, xh, c = (int(v) for v in np.unravel_index(i, SIZES))
        x, y, z, c = move(2 * xh + xl, y, z, c)
        pairs.append((i, int(np.ravel_multi_index((x % 2, z, y, x // 2, c), SIZES))))
    return lax.ppermute(array, AXES, pairs)


def shift_x(array, k):
    return permute(array, lambda x, y, z, c: ((x + k) % 4, y, z, c))


def shift_y(array, k):
    return permute(array, lambda x, y, z, c: (x, (y + k) % 4, z, c))


def shift_z(array, k):
    return permute(array, lambda x, y, z, c: (x, y, (z + k) % 8, c))


def swap_core(array):
    return permute(array, lambda x, y, z, c: (x, y, z, 1 - c))


def call(kernel, in_specs, out_shape, out_specs, scratch=(), flops=0, size=0, limit=48):
    return pl.pallas_call(
        kernel,
        in_specs=in_specs,
        out_specs=out_specs,
        out_shape=out_shape,
        scratch_shapes=scratch,
        cost_estimate=pl.CostEstimate(flops=flops, bytes_accessed=size, transcendentals=0),
        compiler_params=pltpu.CompilerParams(vmem_limit_bytes=limit << 20),
    )


def place():
    x = 2 * lax.axis_index("xh") + lax.axis_index("xl")
    return x, lax.axis_index("y"), lax.axis_index("z"), lax.axis_index("core")


def prep_kernel(q_ref, k_ref, v_ref, *refs):
    x, _, _, _ = place()
    outs, sems = refs[:4], refs[4]
    copies = []
    for s in (1, 2, 3, 0):
        h = lax.rem(x + s, 4)
        start = pl.multiple_of(h * HEAD, HEAD)
        for g in range(GROUP):
            column = pl.multiple_of(h * (GROUP * HEAD) + g * HEAD, HEAD)
            copies.append((q_ref.at[:, pl.ds(column, HEAD)], outs[s].at[pl.ds(g * BLOCK, BLOCK)]))
        copies.append((k_ref.at[:, pl.ds(start, HEAD)], outs[s].at[pl.ds(ROWS, BLOCK)]))
        copies.append((v_ref.at[:, pl.ds(start, HEAD)], outs[s].at[pl.ds(ROWS + BLOCK, BLOCK)]))
    copies = [pltpu.make_async_copy(a, b, sems.at[n]) for n, (a, b) in enumerate(copies)]
    for copy in copies:
        copy.start()
    for copy in copies:
        copy.wait()


def lists_kernel(mask_ref, order_ref, info_ref):
    x, y, z, c = place()
    slots = lax.broadcasted_iota(i32, (1, 256), 1)
    order = order_ref[...]

    def slot(x, y, z, c):
        return lax.rem(x, 2) * 128 + z * 16 + y * 4 + lax.div(x, 2) * 2 + c

    def kv_slot(x, y, z, c):
        return (y * 4 + lax.div(x, 2) * 2 + c) * 16 + lax.rem(x, 2) * 8 + z

    i = lax.broadcasted_iota(i32, (16, 1), 0)
    qx = lax.rem(x - lax.rem(i, 4) + 4, 4)
    qy = lax.rem(y - lax.div(i, 4) + 4, 4)
    q_slot = slot(qx, qy, z, c)
    j = lax.broadcasted_iota(i32, (64, 1), 0)
    unit = lax.div(j, 4)
    zs = jnp.zeros_like(unit)
    cs = jnp.zeros_like(unit)
    for n, (k, other) in enumerate(UNITS):
        zs = jnp.where(unit == n, k, zs)
        cs = jnp.where(unit == n, other, cs)
    kc = lax.rem(c + cs, 2)
    k_slot = kv_slot(lax.rem(x - lax.rem(j, 4) + 4, 4), y, lax.rem(z - zs + 8, 8), kc)

    def one_hot(slot_col):
        block = jnp.sum(jnp.where(slots == slot_col, order, 0), axis=1, keepdims=True)
        return jnp.where(slots == block, 1.0, 0.0).astype(bf16)

    q_hot, k_hot = one_hot(q_slot), one_hot(k_slot)
    rows = jnp.dot(q_hot, mask_ref[...].astype(f32).astype(bf16), preferred_element_type=f32)
    contract = (((1,), (1,)), ((), ()))
    opened = lax.dot_general(rows.astype(bf16), k_hot, contract, preferred_element_type=f32)
    same = lax.dot_general(q_hot, k_hot, contract, preferred_element_type=f32)
    off = opened * (1.0 - same)
    first = lax.broadcasted_iota(i32, (64, 64), 0)
    second = lax.broadcasted_iota(i32, (64, 64), 1)
    below = jnp.where(first < second, 1.0, 0.0).astype(bf16)
    rank = jnp.dot(off.astype(bf16), below, preferred_element_type=f32)
    lane = lax.broadcasted_iota(i32, (16, LANES), 1)
    lanes = lane.astype(f32)
    target = qy * 4 + lax.rem(qx, 2) * 2 + lax.div(qx, 2)
    for ref, low, high in ((info_ref, 0, 64),):
        n_off = jnp.sum(off[:, low:high], axis=1, keepdims=True)
        n_dia = jnp.sum(same[:, low:high], axis=1, keepdims=True)
        pos = jnp.where(same > 0.5, n_off, jnp.where(off > 0.5, rank, 999.0))
        out = jnp.zeros((16, LANES), f32)
        for n in range(low, high):
            out = out + jnp.where(pos[:, n : n + 1] == lanes, float(n - low), 0.0)
        out = jnp.where(lane == CNT, n_off + n_dia, out)
        out = jnp.where(lane == DIA, n_dia, out)
        ref[:16, :] = jnp.where(lane == DST, target, out.astype(i32))
        ref[16:, :] = jnp.zeros((8, LANES), i32)


def attend_kernel(kv_sizes, info, *refs):
    n_kv = len(kv_sizes)
    q_in, kv_in, refs = refs[:4], refs[4 : 4 + n_kv], refs[4 + n_kv :]
    o_ref, m_s, l_s, acc_s, q_s, kv_s, work_q, work_g, half_q, half_g, sems = refs
    copies = [(q_in[t], q_s.at[pl.ds(t * 4, 4)]) for t in range(4)]
    for n in range(n_kv):
        copies.append((kv_in[n], kv_s.at[pl.ds(sum(kv_sizes[:n]), kv_sizes[n])]))
    copies = [pltpu.make_async_copy(a, b, sems.at[n]) for n, (a, b) in enumerate(copies)]
    for copy in copies:
        copy.start()

    def fill(qb, carry):
        t, u = carry
        groups = jnp.maximum(info[qb, CNT] - 1, 0) // HALF

        def put(g, t):
            work_q[t] = qb
            work_g[t] = g * TILES
            return t + 1

        half_q[u] = qb
        half_g[u] = jnp.maximum(groups - 1, 0) * HALF
        return lax.fori_loop(0, groups // 2, put, t), u + lax.rem(groups, 2)

    items, halves = lax.fori_loop(0, 16, fill, (0, 0))
    for u in range(UNROLL - 1):
        work_q[items + u] = 16
        work_g[items + u] = 0
    for u in range(HALF_UNROLL - 1):
        half_q[halves + u] = 16
        half_g[halves + u] = 0
    for copy in copies:
        copy.wait()
    q_s[16] = q_s[0]

    row = lax.broadcasted_iota(i32, (BLOCK, ROWS), 0)
    ahead = row - lax.rem(lax.broadcasted_iota(i32, (BLOCK, ROWS), 1), BLOCK)

    def tiles(qb, base, count, part):
        rows = pl.ds(part * BLOCK, BLOCK)
        return jnp.concatenate([kv_s[info[qb, base + n], rows, :] for n in range(count)], axis=0)

    def scores(qb, base, count):
        return lax.dot_general(
            tiles(qb, base, count, 0), q_s[qb], (((1,), (1,)), ((), ())), preferred_element_type=f32
        )

    def weighted(qb, base, count, p):
        return lax.dot_general(
            tiles(qb, base, count, 1), p, (((0,), (0,)), ((), ())), preferred_element_type=f32
        )

    def masked(s, qb, base):
        n, dia = info[qb, CNT], info[qb, DIA]
        parts = []
        for i in range(HALF):
            limit = jnp.where(base + i < n - dia, 1000, jnp.where(base + i < n, 0, -1000))
            parts.append(jnp.where(ahead <= limit, s[i * BLOCK : (i + 1) * BLOCK], NEG))
        return jnp.concatenate(parts, axis=0)

    def pipeline(items, weigh, store):
        s, p = scores(*items[0]), None
        for n, item in enumerate(items):
            ahead_s = scores(*items[n + 1]) if n + 1 < len(items) else None
            if p is not None:
                store(items[n - 1][0], weighted(*items[n - 1], p))
            p, s = weigh(s, *item).astype(bf16), ahead_s
        store(items[-1][0], weighted(*items[-1], p))

    def weigh_last(s, qb, base, count):
        s = masked(s, qb, base)
        m = jnp.max(s, axis=0, keepdims=True) * LOG2E_SCALE
        p = jnp.exp2(s * LOG2E_SCALE - m)
        m_s[qb] = m
        l_s[qb] = jnp.where(info[qb, CNT] > 0, jnp.sum(p, axis=0, keepdims=True), 0.0)
        return p

    def store_last(qb, value):
        acc_s[qb] = value

    def last(t, carry):
        items = []
        for u in range(LASTU):
            qb = t * LASTU + u
            items.append((qb, jnp.maximum(info[qb, CNT] - 1, 0) // HALF * HALF, HALF))
        pipeline(items, weigh_last, store_last)
        return carry

    lax.fori_loop(0, 16 // LASTU, last, 0)

    def weigh_full(s, qb, base, count):
        p = jnp.exp2(s * LOG2E_SCALE - m_s[qb])
        l_s[qb] += jnp.sum(p, axis=0, keepdims=True)
        return p

    def store_full(qb, value):
        acc_s[qb] += value

    def full(start, count):
        items = [(work_q[start + u], work_g[start + u], TILES) for u in range(count)]
        pipeline(items, weigh_full, store_full)

    def half(t, carry):
        at = [t * HALF_UNROLL + u for u in range(HALF_UNROLL)]
        pipeline([(half_q[n], half_g[n], HALF) for n in at], weigh_full, store_full)
        return carry

    def full_step(t, carry):
        full(t * UNROLL, UNROLL)
        return carry

    m_s[16] = jnp.zeros((1, ROWS), f32)
    steps = (items + UNROLL // 2 - 1) // UNROLL
    lax.fori_loop(0, steps, full_step, 0)

    @pl.when(items > steps * UNROLL)
    def _():
        full(steps * UNROLL, UNROLL // 2)

    lax.fori_loop(0, (halves + HALF_UNROLL - 1) // HALF_UNROLL, half, 0)


    def safe(qb, carry):
        def step(g, state):
            m, l, acc = state
            s = masked(scores(qb, g * HALF, HALF), qb, g * HALF)
            m_new = jnp.maximum(m, jnp.max(s, axis=0, keepdims=True) * LOG2E_SCALE)
            p = jnp.exp2(s * LOG2E_SCALE - m_new)
            fade = jnp.exp2(m - m_new)
            l = l * fade + jnp.sum(p, axis=0, keepdims=True)
            return m_new, l, acc * fade + weighted(qb, g * HALF, HALF, p.astype(bf16))

        start = (jnp.full((1, ROWS), NEG), jnp.zeros((1, ROWS), f32), jnp.zeros((HEAD, ROWS), f32))
        m_s[qb], l_s[qb], acc_s[qb] = lax.fori_loop(
            0, (info[qb, CNT] + HALF - 1) // HALF, step, start
        )
        return carry

    @pl.when(jnp.logical_not(jnp.max(l_s[:16]) < 1e30))
    def _():
        lax.fori_loop(0, 16, safe, 0)

    def finish(qb):
        l = l_s[qb]
        some = l > 0
        inverse = jnp.where(some, 1.0 / l, 0.0)
        target = info[qb, DST]
        o = (acc_s[qb] * inverse).astype(bf16)
        lse = jnp.where(some, m_s[qb] * math.log(2.0) + jnp.log(l), NEG)
        high = lse.astype(bf16).astype(f32)
        mid = (lse - high).astype(bf16).astype(f32)
        low = lse - high - mid
        at = lax.broadcasted_iota(i32, (TAIL, LANES), 0)
        tail = jnp.zeros((TAIL, LANES), f32)
        for side in range(2):
            lanes = slice(side * LANES, (side + 1) * LANES)
            o_ref[target, side * HEAD : (side + 1) * HEAD, :] = o[:, lanes]
            for n, term in enumerate((high, mid, low)):
                tail = jnp.where(at == 2 * n + side, term[:, lanes], tail)
        o_ref[target, 2 * HEAD :, :] = tail.astype(bf16)

    def finish_some(t, carry):
        for u in range(FIN):
            finish(t * FIN + u)
        return carry

    lax.fori_loop(0, 16 // FIN, finish_some, 0)


def combine_kernel(in_ref, out_ref, lse_ref):
    for h in range(4):
        src = [c * 4 + (h % 2) * 2 + h // 2 for c in range(4)]
        for side in range(2):
            lses = []
            for s in src:
                tail = in_ref[s, 2 * HEAD :, :].astype(f32)
                lses.append(sum(tail[2 * n + side : 2 * n + side + 1] for n in range(3)))
            top = jnp.maximum(jnp.maximum(lses[0], lses[1]), jnp.maximum(lses[2], lses[3]))
            weights = [jnp.exp(lse - top) for lse in lses]
            total = weights[0] + weights[1] + weights[2] + weights[3]
            inverse = 1.0 / total
            rows = slice(side * HEAD, (side + 1) * HEAD)
            o = sum(in_ref[s, rows, :].astype(f32) * (w * inverse) for s, w in zip(src, weights))
            o = o.T.astype(bf16)
            lse = top + jnp.log(total)
            for g in range(2):
                part = slice(g * BLOCK, (g + 1) * BLOCK)
                head = h * GROUP + side * 2 + g
                out_ref[:, head * HEAD : (head + 1) * HEAD] = o[part]
                lse_ref[head : head + 1, :] = lse[:, part]


def attend(info, qs, kv):
    sizes = tuple(a.shape[0] for a in kv)
    blocks = sum(sizes)
    return call(
        functools.partial(attend_kernel, sizes),
        [SMEM] + [ANY] * (4 + len(kv)),
        jax.ShapeDtypeStruct((16, 2 * HEAD + TAIL, LANES), bf16),
        VMEM,
        [
            pltpu.VMEM((17, 1, ROWS), f32),
            pltpu.VMEM((17, 1, ROWS), f32),
            pltpu.VMEM((17, HEAD, ROWS), f32),
            pltpu.VMEM((17, ROWS, HEAD), bf16),
            pltpu.VMEM((blocks, 2 * BLOCK, HEAD), bf16),
            pltpu.SMEM((2 * blocks + UNROLL,), i32),
            pltpu.SMEM((2 * blocks + UNROLL,), i32),
            pltpu.SMEM((16 + HALF_UNROLL,), i32),
            pltpu.SMEM((16 + HALF_UNROLL,), i32),
            pltpu.SemaphoreType.DMA((4 + len(kv),)),
        ],
        flops=blocks * 200_000_000,
        size=8_000_000,
    )(info, *qs, *kv)


def body(queries, keys, values, tile_mask, slot_order):
    with jax.named_scope("prep"):
        piece = jax.ShapeDtypeStruct((ROWS + 2 * BLOCK, HEAD), bf16)
        pieces = call(
            prep_kernel,
            [pl.BlockSpec(memory_space=pltpu.HBM)] * 3,
            [piece] * 4,
            [VMEM] * 4,
            [pltpu.SemaphoreType.DMA((24,))],
        )(queries, keys, values)
    with jax.named_scope("lists"):
        table = jax.ShapeDtypeStruct((24, LANES), i32)
        info = call(lists_kernel, [VMEM, VMEM], table, VMEM)(tile_mask, slot_order.reshape(1, 256))
    with jax.named_scope("heads"):
        pieces = [pieces[0]] + [shift_x(pieces[s], s) for s in (1, 2, 3)]
        pieces, info = lax.optimization_barrier((pieces, info))
        own_kv = jnp.stack([p[ROWS:] for p in pieces])
        own_q = jnp.stack([p[:ROWS] for p in pieces])
    with jax.named_scope("gather"):
        qs = [own_q] + [shift_y(own_q, t) for t in (1, 2, 3)]
        kv = {0: own_kv, 1: shift_z(own_kv, 1), 7: shift_z(own_kv, 7)}
        kv[2] = shift_z(kv[1], 1)
        kv[6] = shift_z(kv[7], 7)
        kv[3] = shift_z(kv[2], 1)
        kv[5] = shift_z(kv[6], 7)
        kv[4] = shift_z(kv[2], 2)
        kv, qs = lax.optimization_barrier((kv, qs))
        own = jnp.concatenate([kv[s] for s in Z_ORDER])
        other = swap_core(own)
    with jax.named_scope("attend"):
        partial = attend(info, qs, [own, other])
    with jax.named_scope("exchange"):
        parts = lax.all_to_all(partial, ("y", "xl", "xh"), split_axis=0, concat_axis=0, tiled=True)
    with jax.named_scope("combine"):
        return call(
            combine_kernel,
            [VMEM],
            [jax.ShapeDtypeStruct((BLOCK, 16 * HEAD), bf16), jax.ShapeDtypeStruct((16, BLOCK), f32)],
            [VMEM, VMEM],
        )(parts)


def solution(mesh):
    fine = Mesh(mesh.devices.reshape(SIZES), AXES)
    by_query, by_key = AXES, ("y", "xh", "core", "xl", "z")
    return jax.shard_map(
        body,
        mesh=fine,
        in_specs=(P(by_query, None), P(by_key, None), P(by_key, None), P(), P()),
        out_specs=(P(by_query, None), P(None, by_query)),
        check_vma=False,
    )
```
